256 devices in a mesh: owner: 32 (over x, y, core), aux: 8 (over z).
Axes of the slice: x: 4, y: 4, z: 8, core: 2. Of those that a mesh axis runs over, the one named last changes fastest.
Arguments:
- fit_left: bfloat16 [128, 256, 128, 128], P('owner', 'aux'), may hold values from -0.5 to 0.5
- fit_right: bfloat16 [128, 256, 128, 128], P('owner', 'aux'), may hold values from -0.03125 to 0.03125
- t2_tiles: bfloat16 [128, 8, 128, 128], P('owner'), may hold values from -6 to 6
- task_count: int32 [32], P('owner'), may hold values from 1 to 4, as said below
- task_target: int32 [128], P('owner'), may hold values from 0 to 31
Outputs:
- residual: bfloat16 [32, 8, 128, 128], P('owner', 'aux')
The draws below stay inside these ranges and needn't reach their ends.
Inputs may be any that keep to these rules, and one draw needn't show every extreme that they name: task_count equals 4 on at least one index of owner.
All inputs are finite; a program needn't handle non-finite values.
Results may differ from the reference program's by a relative error of at most 0.0049.
Values may be sent and summed in bfloat16 or wider, within the bound.
A program may use at most 128 MiB of HBM per device.

```python
import jax
import jax.numpy as jnp
from jax import lax

TILE = 128
PAIRS = 8
TASK_DEV = 4
NAUX = 256
TASKS = 128
N_OWNER = 32


def draw_task_count(key, part):
    key = jax.random.fold_in(key, 7)
    key_one, key_two = jax.random.split(key)
    raw_draw = jax.random.randint(key_one, (N_OWNER,), 0, TASK_DEV + 1)
    load_list = 1 + raw_draw * raw_draw * (TASK_DEV - 1) // (TASK_DEV * TASK_DEV)
    heaviest = jax.random.randint(key_two, (), 0, N_OWNER)
    return jnp.where(jnp.arange(N_OWNER) == heaviest, TASK_DEV, load_list).astype(jnp.int32)


def set_ends(result, stream_key, smallest, largest):
    extent = result.shape
    spot = [jax.random.randint(jax.random.fold_in(stream_key, axis), (), 0, extent[axis]) for axis in range(len(extent))]
    result = result.at[tuple(spot)].set(smallest)
    longest = extent.index(max(extent))
    spot[longest] = (spot[longest] + 1) % extent[longest]
    return result.at[tuple(spot)].set(largest)


def steps_of(rng, shape, cuts, least, high):
    def one(dim, parts):
        heights = jax.random.uniform(jax.random.fold_in(jax.random.fold_in(rng, 6), dim), (parts,), jnp.float32, least / len(cuts), high / len(cuts))
        return jnp.repeat(jnp.exp(heights), shape[dim] // parts).reshape((-1,) + (1,) * (len(shape) - dim - 1))

    gain = one(*cuts[0])
    for cut in cuts[1:]:
        gain = gain * one(*cut)
    return gain


def normal_values(key, extent, spread, reach, shards=(), kind=jnp.bfloat16):
    gain = steps_of(key, extent, shards, -0.22, 0.18) if shards else 1.0
    result = jax.random.normal(key, extent, jnp.float32) * spread * gain
    return jnp.minimum(jnp.maximum(result, -reach), reach).astype(kind)


def setup_inputs(seed: int = 0) -> dict:
    key_of = jax.random.split(jax.random.key(seed), 6)
    fit_left = normal_values(key_of[0], (TASKS, NAUX, TILE, TILE), TILE ** -0.5, 0.5, ((0, 32), (1, 8)))
    fit_right = normal_values(key_of[1], (TASKS, NAUX, TILE, TILE), (NAUX * TILE) ** -0.5, 0.03125, ((0, 32), (1, 8)))
    t2_tiles = normal_values(key_of[2], (TASKS, PAIRS, TILE, TILE), 1.0, 6.0, ((0, 32),))
    task_count = draw_task_count(jax.random.fold_in(key_of[5], 71), 0)
    task_target = set_ends(jax.random.randint(key_of[4], (TASKS,), 0, N_OWNER), jax.random.fold_in(key_of[4], 1), 0, N_OWNER - 1).astype(jnp.int32)
    return dict(fit_left=fit_left, fit_right=fit_right, t2_tiles=t2_tiles, task_count=task_count, task_target=task_target)


def ladder_term(left_fit, right_fit, amplitudes):
    halves = jnp.einsum('qac,icd->qiad', left_fit, amplitudes, preferred_element_type=jnp.float32).astype(jnp.bfloat16)
    return jnp.einsum('qiad,qbd->iab', halves, right_fit, preferred_element_type=jnp.float32)


def reference(fit_left, fit_right, t2_tiles, task_count, task_target):
    summed = jnp.zeros((N_OWNER, PAIRS, TILE, TILE), jnp.float32)

    def step(accum, position):
        live_flag = (position % TASK_DEV) < task_count[position // TASK_DEV]

        def add_term(inner):
            return inner.at[task_target[position]].add(ladder_term(fit_left[position], fit_right[position], t2_tiles[position]))

        return lax.cond(live_flag, add_term, lambda inner: inner, accum), None

    summed, unused = lax.scan(step, summed, jnp.arange(N_OWNER * TASK_DEV, dtype=jnp.int32))
    return summed.astype(jnp.bfloat16)
```

```python
import functools

import jax
import jax.numpy as jnp
from jax import lax
from jax.experimental import pallas as pl
from jax.experimental.pallas import tpu as pltpu
from jax.sharding import PartitionSpec as P

MESH = pl.DeviceIdType.MESH
f32, bf16 = jnp.float32, jnp.bfloat16
FAR = (4, 3, 5, 1)
NEAR = (2, 6, 7, 0)


def kernel(
    sizes, count_ref, target_ref, left_hbm, right_hbm, t2_hbm, out_ref,
    left, right, t2, half, term, far_out, relay, relay_info, near_out, near_in, info, own, blocks_out, blocks_in,
    load_sem, far_send, relay_recv, near_send, near_recv, info_send, info_recv, block_send, block_recv,
):
    owners, aux, parts, tasks, naux, tile = sizes
    rows = tile // parts
    me = lax.axis_index("owner")
    z = lax.axis_index("aux")
    part = lax.rem(me, parts)

    def at(dz, m):
        return ((me // parts) * parts + lax.rem(part + m, parts), lax.rem(z + dz, aux))

    def loads(g):
        return [
            pltpu.make_async_copy(t2_hbm.at[g], t2.at[g], load_sem.at[0, g]),
            pltpu.make_async_copy(left_hbm.at[g], left.at[g], load_sem.at[1, g]),
            pltpu.make_async_copy(right_hbm.at[g], right.at[g], load_sem.at[2, g]),
        ]

    for g in range(tasks):
        for copy in loads(g):
            copy.start()

    barrier = pltpu.get_barrier_semaphore()
    for dz in (1, 2, 6, 7):
        for m in range(parts):
            pl.semaphore_signal(barrier, inc=1, device_id=at(dz, m), device_id_type=MESH)

    def greet(r, carry):
        pl.semaphore_signal(
            barrier, inc=1, device_id=(lax.rem(me + r, owners), z), device_id_type=MESH
        )
        return carry

    lax.fori_loop(1, owners, greet, 0)

    rows_of_info = [
        jnp.full((1, tile), jnp.where(g < count_ref[0], target_ref[g], -1), jnp.int32)
        for g in range(tasks)
    ]
    info[0] = jnp.concatenate(rows_of_info + [jnp.full((8 - tasks, tile), -1, jnp.int32)], axis=0)

    def info_copy(m):
        return pltpu.make_async_remote_copy(
            src_ref=info.at[0], dst_ref=info.at[m], send_sem=info_send.at[m], recv_sem=info_recv.at[m],
            device_id=at(0, m), device_id_type=MESH,
        )

    def relay_copy(p, g):
        dz = (2 + 4 * (g // 2), 1, 7)[p]
        return pltpu.make_async_remote_copy(
            src_ref=far_out.at[p, g], dst_ref=relay.at[p, g], send_sem=far_send.at[p, g],
            recv_sem=relay_recv.at[p, g], device_id=at(dz, 0), device_id_type=MESH,
        )

    def near_copy(s, m, g):
        dz = (1, 2, 6, 7, 0)[s]
        away = lax.rem(part + m, parts)
        return pltpu.make_async_remote_copy(
            src_ref=near_out.at[s, g, pl.ds(pl.multiple_of(away * rows, rows), rows)],
            dst_ref=near_in.at[s, m, g], send_sem=near_send.at[s, m, g],
            recv_sem=near_recv.at[s, m, g], device_id=at(dz, m), device_id_type=MESH,
        )

    def block_copy(r):
        return pltpu.make_async_remote_copy(
            src_ref=blocks_out.at[r], dst_ref=blocks_in.at[r], send_sem=block_send.at[r],
            recv_sem=block_recv.at[r], device_id=(lax.rem(me + r, owners), z), device_id_type=MESH,
        )

    def multiply(g, near):
        pairs = [lax.rem(z + FAR[p] + near * (NEAR[p] - FAR[p] + aux), aux) for p in range(4)]
        amps = jnp.concatenate([t2[g, pair].T for pair in pairs], axis=0)
        step = 8
        for q in range(0, naux, step):
            block = lax.dot_general(
                amps, left[g, q : q + step].reshape(step * tile, tile), (((1,), (1,)), ((), ())),
                preferred_element_type=f32,
            ).astype(bf16)
            for k in range(step):
                for p in range(4):
                    half[(q + k) * tile : (q + k + 1) * tile, p * tile : (p + 1) * tile] = block[
                        p * tile : (p + 1) * tile, k * tile : (k + 1) * tile
                    ]
        fit = jnp.concatenate([right[g, q] for q in range(naux)], axis=1)
        term[...] = jnp.dot(fit, half[...], preferred_element_type=f32)

    def block_of(p):
        return term[:, p * tile : (p + 1) * tile]

    def send_near(s, g, value):
        near_out[s, g] = value.astype(bf16)
        for m in range(parts):
            if s < 4 or m:
                near_copy(s, m, g).start()

    def unit(u, carry):
        near = u // tasks
        g = lax.rem(u, tasks)

        @pl.when(near == 0)
        def _():
            for copy in loads(g):
                copy.wait()

        multiply(g, near)

        @pl.when(u == 0)
        def _():
            pl.semaphore_wait(barrier, 4 * parts + owners - 1)
            for m in range(1, parts):
                info_copy(m).start()

        @pl.when(near == 0)
        def _():
            for p in range(3):
                far_out[p, g] = block_of(p).astype(bf16)
                relay_copy(p, g).start()
            send_near(0, g, block_of(3))

        @pl.when(near == 1)
        def _():
            for p in range(3):
                relay_copy(p, g).wait_recv()
            extra = relay[0, g].astype(f32)
            up = (g // 2 == 0).astype(f32)
            send_near(1, g, block_of(0) + relay[1, g].astype(f32) + extra * up)
            send_near(2, g, block_of(1) + relay[2, g].astype(f32) + extra * (1.0 - up))
            send_near(3, g, block_of(2))
            send_near(4, g, block_of(3))
            own[g] = term[pl.ds(pl.multiple_of(part * rows, rows), rows), 3 * tile :]

        return carry

    lax.fori_loop(0, 2 * tasks, unit, 0)

    for m in range(1, parts):
        info_copy(m).wait_recv()

    def drain(g, carry):
        for m in range(parts):
            for s in range(5):
                if s < 4 or m:
                    near_copy(s, m, g).wait_recv()
                    value = near_in[s, m, g].astype(f32)
                    total = value if s == 0 else total + value
            if m == 0:
                total = total + own[g]
            relay_info[m, g] = total
        return carry

    lax.fori_loop(0, tasks, drain, 0)

    def gather(r):
        target = lax.rem(me + r, owners)
        total = jnp.zeros((rows, tile), f32)
        for m in range(parts):
            for g in range(tasks):
                hit = jnp.broadcast_to(info[m, g : g + 1, :], (rows, tile)) == target
                total += jnp.where(hit, relay_info[m, g], 0.0)
        return total

    def scatter(r, carry):
        blocks_out[r] = gather(r).astype(bf16)
        block_copy(r).start()
        return carry

    lax.fori_loop(1, owners, scatter, 0)
    term[:, 0:tile] = jnp.zeros((tile, tile), f32)
    term[pl.ds(pl.multiple_of(part * rows, rows), rows), 0:tile] = gather(0)

    def collect(r, carry):
        block_copy(r).wait_recv()
        source = lax.rem(lax.rem(me + owners - r, owners), parts)
        where = pl.ds(pl.multiple_of(source * rows, rows), rows)
        term[where, 0:tile] += blocks_in[r].astype(f32)
        return carry

    lax.fori_loop(1, owners, collect, 0)
    out_ref[0, 0] = term[:, 0:tile].T.astype(bf16)

    for m in range(1, parts):
        info_copy(m).wait_send()

    def finish(g, carry):
        for p in range(3):
            relay_copy(p, g).wait_send()
        for s in range(5):
            for m in range(parts):
                if s < 4 or m:
                    near_copy(s, m, g).wait_send()
        return carry

    lax.fori_loop(0, tasks, finish, 0)

    def finish_blocks(r, carry):
        block_copy(r).wait_send()
        return carry

    lax.fori_loop(1, owners, finish_blocks, 0)


def solution(mesh):
    owners, aux = mesh.shape["owner"], mesh.shape["aux"]
    parts = 2

    def on_device(fit_left, fit_right, t2_tiles, task_count, task_target):
        tasks, naux, tile, _ = fit_left.shape
        pairs = t2_tiles.shape[1]
        rows = tile // parts
        vmem, dma = pltpu.VMEM, pltpu.SemaphoreType.DMA
        return pl.pallas_call(
            functools.partial(kernel, (owners, aux, parts, tasks, naux, tile)),
            out_shape=jax.ShapeDtypeStruct((1, 1, tile, tile), bf16),
            in_specs=[pl.BlockSpec(memory_space=pltpu.SMEM)] * 2 + [pl.BlockSpec(memory_space=pl.ANY)] * 3,
            out_specs=pl.BlockSpec(memory_space=pltpu.VMEM),
            scratch_shapes=[
                vmem((tasks, naux, tile, tile), bf16),
                vmem((tasks, naux, tile, tile), bf16),
                vmem((tasks, pairs, tile, tile), bf16),
                vmem((naux * tile, 4 * tile), bf16),
                vmem((tile, 4 * tile), f32),
                vmem((3, tasks, tile, tile), bf16),
                vmem((3, tasks, tile, tile), bf16),
                vmem((parts, tasks, rows, tile), f32),
                vmem((5, tasks, tile, tile), bf16),
                vmem((5, parts, tasks, rows, tile), bf16),
                vmem((parts, 8, tile), jnp.int32),
                vmem((tasks, rows, tile), f32),
                vmem((owners, rows, tile), bf16),
                vmem((owners, rows, tile), bf16),
                dma((3, tasks)),
                dma((3, tasks)),
                dma((3, tasks)),
                dma((5, parts, tasks)),
                dma((5, parts, tasks)),
                dma((parts,)),
                dma((parts,)),
                dma((owners,)),
                dma((owners,)),
            ],
            compiler_params=pltpu.CompilerParams(
                collective_id=0, has_side_effects=True, vmem_limit_bytes=48 << 20
            ),
            name="ladder",
        )(task_count, task_target, fit_left, fit_right, t2_tiles)

    placed = (
        P("owner", "aux", None, None),
        P("owner", "aux", None, None),
        P("owner", None, None, None),
        P("owner"),
        P("owner"),
    )
    return jax.shard_map(
        on_device,
        mesh=mesh,
        in_specs=placed,
        out_specs=P("owner", "aux", None, None),
        check_vma=False,
    )
```

```python
import functools

import jax
import jax.numpy as jnp
from jax import lax
from jax.experimental import pallas as pl
from jax.experimental.pallas import tpu as pltpu
from jax.sharding import PartitionSpec as P

MESH = pl.DeviceIdType.MESH
f32, bf16 = jnp.float32, jnp.bfloat16
SIDE, CORES, PARTS, CHUNK = 4, 2, 4, 4
OFFSETS = ((4, 3), (5, 1), (2, 6), (7, 0))
NEAR_DZ = (1, 2, 6, 7, 0)
HOLD = 2


def kernel(
    sizes, count_ref, target_ref, left_hbm, right_hbm, t2_hbm, out_ref,
    left, right, t2, half_even, half_odd, term, far_out, relay, near_out, near_in, info, own, blocks, blocks_out,
    blocks_in, total,
    load_sem, left_sem, far_send, relay_recv, near_send, near_recv, info_send, info_recv, block_send, block_recv,
):
    owners, aux, tasks, naux, tile = sizes
    rows = tile // PARTS
    units = tasks * len(OFFSETS)
    slots = owners // PARTS
    me = lax.axis_index("owner")
    z = lax.axis_index("aux")
    x, y, core = me // (SIDE * CORES), lax.rem(me // CORES, SIDE), lax.rem(me, CORES)
    part = core + CORES * lax.rem(x, 2)

    def at(dz, m):
        away = lax.rem(part + m, PARTS)
        there = ((x // 2) * 2 + away // CORES) * (SIDE * CORES) + y * CORES + lax.rem(away, CORES)
        return (there, lax.rem(z + dz, aux))

    def owner_at(m, k):
        dx, dy, dc = 2 * (k // SIDE) + m // CORES, lax.rem(k, SIDE), m % CORES
        return (
            lax.rem(x + dx, SIDE) * (SIDE * CORES) + lax.rem(y + dy, SIDE) * CORES + lax.rem(core + dc, CORES)
        )

    def load_t2(g):
        return pltpu.make_async_copy(t2_hbm.at[g], t2.at[g], load_sem.at[0, g])

    def load_right(g):
        return pltpu.make_async_copy(right_hbm.at[g], right.at[g], load_sem.at[1, g])

    def load_left(g, k):
        part_of = pl.ds(k * (naux // 4), naux // 4)
        return pltpu.make_async_copy(left_hbm.at[g, part_of], left.at[g, part_of], left_sem.at[g, k])

    def start_loads(g):
        load_t2(g).start()
        for k in range(4):
            load_left(g, k).start()
        load_right(g).start()

    start_loads(0)

    barrier = pltpu.get_barrier_semaphore()
    for dz in (1, 2, 6, 7):
        for m in range(PARTS):
            pl.semaphore_signal(barrier, inc=1, device_id=at(dz, m), device_id_type=MESH)

    def greet(r, carry):
        pl.semaphore_signal(
            barrier, inc=1, device_id=(lax.rem(me + r, owners), z), device_id_type=MESH
        )
        return carry

    lax.fori_loop(1, owners, greet, 0)

    rows_of_info = [
        jnp.full((1, tile), jnp.where(g < count_ref[0], target_ref[g], -1), jnp.int32)
        for g in range(tasks)
    ]
    info[0] = jnp.concatenate(rows_of_info + [jnp.full((8 - tasks, tile), -1, jnp.int32)], axis=0)

    def info_copy(m):
        return pltpu.make_async_remote_copy(
            src_ref=info.at[0], dst_ref=info.at[m], send_sem=info_send.at[m], recv_sem=info_recv.at[m],
            device_id=at(0, m), device_id_type=MESH,
        )

    def relay_copy(p, g):
        dz = (2 + 4 * lax.rem(g, 2), 1, 7)[p]
        return pltpu.make_async_remote_copy(
            src_ref=far_out.at[p, g], dst_ref=relay.at[p, g], send_sem=far_send.at[p, g],
            recv_sem=relay_recv.at[p, g], device_id=at(dz, 0), device_id_type=MESH,
        )

    def near_copy(s, m, g):
        away = lax.rem(part + m, PARTS)
        return pltpu.make_async_remote_copy(
            src_ref=near_out.at[s, g, pl.ds(pl.multiple_of(away * rows, rows), rows)],
            dst_ref=near_in.at[s, m, g], send_sem=near_send.at[s, m, g],
            recv_sem=near_recv.at[s, m, g], device_id=at(NEAR_DZ[s], m), device_id_type=MESH,
        )

    def block_copy(m, k):
        return pltpu.make_async_remote_copy(
            src_ref=blocks_out.at[m, k], dst_ref=blocks_in.at[m, k], send_sem=block_send.at[m, k],
            recv_sem=block_recv.at[m, k], device_id=(owner_at(m, k), z), device_id_type=MESH,
        )

    def place(u):
        late, i = u // (2 * tasks), lax.rem(u, 2 * tasks)
        last, j = i // tasks, lax.rem(i, tasks)
        g_late = (1 - last) * (i // 2) + last * (2 + lax.rem(j, 2))
        stage_late = (1 - last) * (3 - lax.rem(i, 2)) + last * (2 + j // 2)
        g = (1 - late) * (u // 2) + late * g_late
        stage = (1 - late) * lax.rem(u, 2) + late * stage_late
        return g, stage

    def amplitudes(u):
        g, stage = place(u)
        found = []
        for p in range(2):
            a, b, c, d = (pair[p] for pair in OFFSETS)
            low = a + stage * (b - a)
            high = c + (stage - 2) * (d - c)
            offset = low + (stage // 2) * (high - low)
            found.append(t2[g, lax.rem(z + offset, aux)].T)
        return jnp.concatenate(found, axis=0)

    def first(half, u, amps, q):
        g, _ = place(u)
        block = lax.dot_general(
            amps, left[g, pl.ds(q, CHUNK)].reshape(CHUNK * tile, tile), (((1,), (1,)), ((), ())),
            preferred_element_type=f32,
        ).astype(bf16)
        for k in range(CHUNK):
            for p in range(2):
                half[(q + k) * tile : (q + k + 1) * tile, p * tile : (p + 1) * tile] = block[
                    p * tile : (p + 1) * tile, k * tile : (k + 1) * tile
                ]

    def second(half, u, q):
        g, _ = place(u)
        fit = jnp.concatenate([right[g, q + k] for k in range(CHUNK)], axis=1)
        value = jnp.dot(fit, half[q * tile : (q + CHUNK) * tile, :], preferred_element_type=f32)
        if q == 0:
            term[...] = value
        else:
            term[...] += value

    def multiply(half_new, half_old, u):
        amps = amplitudes(u + 1)
        for q in range(0, naux, CHUNK):
            first(half_new, u + 1, amps, q)
            second(half_old, u, q)

    def send(u, carry):
        g, stage = place(u)

        @pl.when(stage == 0)
        def _():
            relay_copy(0, g).start()
            relay_copy(1, g).start()

        @pl.when(stage == 1)
        def _():
            relay_copy(2, g).start()
            for m in range(PARTS):
                near_copy(0, m, g).start()

        @pl.when(stage == 2)
        def _():
            for m in range(PARTS):
                near_copy(1, m, g).start()
                near_copy(2, m, g).start()

        @pl.when(stage == 3)
        def _():
            for m in range(PARTS):
                near_copy(3, m, g).start()
            for m in range(1, PARTS):
                near_copy(4, m, g).start()

        return carry

    def deliver(u):
        g, stage = place(u)
        lower, upper = slice(0, tile), slice(tile, 2 * tile)

        @pl.when(stage == 0)
        def _():
            far_out[0, g] = term[:, lower].astype(bf16)
            far_out[1, g] = term[:, upper].astype(bf16)

        @pl.when(stage == 1)
        def _():
            far_out[2, g] = term[:, lower].astype(bf16)
            near_out[0, g] = term[:, upper].astype(bf16)

        @pl.when(stage == 2)
        def _():
            for p in range(3):
                relay_copy(p, g).wait_recv()
            extra = relay[0, g].astype(f32)
            up = (lax.rem(g, 2) == 0).astype(f32)
            near_out[1, g] = (term[:, lower] + relay[1, g].astype(f32) + extra * up).astype(bf16)
            near_out[2, g] = (term[:, upper] + relay[2, g].astype(f32) + extra * (1.0 - up)).astype(bf16)

        @pl.when(stage == 3)
        def _():
            near_out[3, g] = term[:, lower].astype(bf16)
            near_out[4, g] = term[:, upper].astype(bf16)
            own[g] = term[pl.ds(pl.multiple_of(part * rows, rows), rows), upper]

        if isinstance(u, int):
            send(u, 0)
        else:
            @pl.when(u == HOLD)
            def _():
                pl.semaphore_wait(barrier, 4 * PARTS + owners - 1)
                for m in range(1, PARTS):
                    info_copy(m).start()
                lax.fori_loop(0, HOLD, send, 0)

            @pl.when(u >= HOLD)
            def _():
                send(u, 0)

    def pair_of_units(v, carry):
        @pl.when(v < tasks)
        def _():
            load_right(v).wait()

        multiply(half_odd, half_even, 2 * v)
        deliver(2 * v)

        @pl.when(v < tasks - 1)
        def _():
            load_t2(v + 1).wait()
            for k in range(4):
                load_left(v + 1, k).wait()

        @pl.when(v < tasks - 2)
        def _():
            start_loads(v + 2)

        multiply(half_even, half_odd, 2 * v + 1)
        deliver(2 * v + 1)
        return carry

    load_t2(0).wait()
    amps = amplitudes(0)
    for q in range(0, naux, CHUNK):
        if q % (naux // 4) == 0:
            load_left(0, q // (naux // 4)).wait()
        if q == naux - naux // 4:
            start_loads(1)
        first(half_even, 0, amps, q)
    lax.fori_loop(0, units // 2 - 1, pair_of_units, 0)
    multiply(half_odd, half_even, units - 2)
    deliver(units - 2)
    for q in range(0, naux, CHUNK):
        second(half_odd, units - 1, q)
    deliver(units - 1)

    for m in range(1, PARTS):
        info_copy(m).wait_recv()

    def shares(g):
        found = []
        for m in range(PARTS):
            for s in range(5):
                if s < 4 or m:
                    near_copy(s, m, g).wait_recv()
        for m in range(PARTS):
            value = own[g] if m == 0 else near_in[4, m, g].astype(f32)
            for s in range(4):
                value += near_in[s, m, g].astype(f32)
            found.append(value)
        return found

    def add_shares(g, found, m, k):
        target = owner_at(m, k)
        value = None
        for n in range(PARTS):
            hit = jnp.broadcast_to(info[n, pl.ds(g, 1), :], (rows, tile)) == target
            part_of = jnp.where(hit, found[n], 0.0)
            value = part_of if value is None else value + part_of
        return value

    order = [(m, k) for k in (6, 5, 7, 4, 2, 1, 3, 0) for m in (2, 3, 1, 0)]

    def accumulate(g, carry):
        found = shares(g)
        for m, k in order:
            blocks[m, k] += add_shares(g, found, m, k)
        return carry

    blocks[...] = jnp.zeros_like(blocks)
    lax.fori_loop(0, tasks - 1, accumulate, 0)
    found = shares(tasks - 1)
    for m, k in order:
        value = blocks[m, k] + add_shares(tasks - 1, found, m, k)
        if m or k:
            blocks_out[m, k] = value.astype(bf16)
            block_copy(m, k).start()
        else:
            blocks[0, 0] = value

    for m in range(PARTS):
        for k in range(slots):
            if m or k:
                block_copy(m, k).wait_recv()
        value = None
        for k in range(slots):
            one = blocks[0, 0] if m == 0 and k == 0 else blocks_in[m, k].astype(f32)
            value = one if value is None else value + one
        source = lax.rem(core + m % CORES, CORES) + CORES * lax.rem(x + m // CORES, 2)
        total[pl.ds(pl.multiple_of(source * rows, rows), rows), :] = value
    out_ref[0, 0] = total[...].T.astype(bf16)

    for m in range(1, PARTS):
        info_copy(m).wait_send()

    def finish(g, carry):
        for p in range(3):
            relay_copy(p, g).wait_send()
        for s in range(5):
            for m in range(PARTS):
                if s < 4 or m:
                    near_copy(s, m, g).wait_send()
        return carry

    lax.fori_loop(0, tasks, finish, 0)
    for m in range(PARTS):
        for k in range(slots):
            if m or k:
                block_copy(m, k).wait_send()


def solution(mesh):
    owners, aux = mesh.shape["owner"], mesh.shape["aux"]

    def on_device(fit_left, fit_right, t2_tiles, task_count, task_target):
        tasks, naux, tile, _ = fit_left.shape
        pairs = t2_tiles.shape[1]
        rows = tile // PARTS
        slots = owners // PARTS
        vmem, dma = pltpu.VMEM, pltpu.SemaphoreType.DMA
        return pl.pallas_call(
            functools.partial(kernel, (owners, aux, tasks, naux, tile)),
            out_shape=jax.ShapeDtypeStruct((1, 1, tile, tile), bf16),
            in_specs=[pl.BlockSpec(memory_space=pltpu.SMEM)] * 2 + [pl.BlockSpec(memory_space=pl.ANY)] * 3,
            out_specs=pl.BlockSpec(memory_space=pltpu.VMEM),
            scratch_shapes=[
                vmem((tasks, naux, tile, tile), bf16),
                vmem((tasks, naux, tile, tile), bf16),
                vmem((tasks, pairs, tile, tile), bf16),
                vmem((naux * tile, 2 * tile), bf16),
                vmem((naux * tile, 2 * tile), bf16),
                vmem((tile, 2 * tile), f32),
                vmem((3, tasks, tile, tile), bf16),
                vmem((3, tasks, tile, tile), bf16),
                vmem((5, tasks, tile, tile), bf16),
                vmem((5, PARTS, tasks, rows, tile), bf16),
                vmem((PARTS, 8, tile), jnp.int32),
                vmem((tasks, rows, tile), f32),
                vmem((PARTS, slots, rows, tile), f32),
                vmem((PARTS, slots, rows, tile), bf16),
                vmem((PARTS, slots, rows, tile), bf16),
                vmem((tile, tile), f32),
                dma((2, tasks)),
                dma((tasks, 4)),
                dma((3, tasks)),
                dma((3, tasks)),
                dma((5, PARTS, tasks)),
                dma((5, PARTS, tasks)),
                dma((PARTS,)),
                dma((PARTS,)),
                dma((PARTS, slots)),
                dma((PARTS, slots)),
            ],
            compiler_params=pltpu.CompilerParams(
                collective_id=0, has_side_effects=True, vmem_limit_bytes=62 << 20
            ),
            name="ladder",
        )(task_count, task_target, fit_left, fit_right, t2_tiles)

    placed = (
        P("owner", "aux", None, None),
        P("owner", "aux", None, None),
        P("owner", None, None, None),
        P("owner"),
        P("owner"),
    )
    return jax.shard_map(
        on_device,
        mesh=mesh,
        in_specs=placed,
        out_specs=P("owner", "aux", None, None),
        check_vma=False,
    )
```

```python
import functools

import jax
import jax.numpy as jnp
from jax import lax
from jax.experimental import pallas as pl
from jax.experimental.pallas import tpu as pltpu
from jax.sharding import PartitionSpec as P

MESH = pl.DeviceIdType.MESH
f32, bf16 = jnp.float32, jnp.bfloat16
SIDE, CORES, PARTS, CHUNK = 4, 2, 4, 4
OFFSETS = ((4, 3), (5, 1), (2, 6), (7, 0))
NEAR_DZ = (1, 2, 6, 7, 0)


def kernel(
    sizes, count_ref, target_ref, left_hbm, right_hbm, t2_hbm, out_ref,
    left, right, t2, half_even, half_odd, term, far_out, relay, near_out, near_in, info, own, blocks, blocks_out,
    blocks_in, total,
    load_sem, left_sem, far_send, relay_recv, near_send, near_recv, info_send, info_recv, block_send, block_recv,
):
    owners, aux, tasks, naux, tile = sizes
    rows = tile // PARTS
    units = tasks * len(OFFSETS)
    slots = owners // PARTS
    me = lax.axis_index("owner")
    z = lax.axis_index("aux")
    x, y, core = me // (SIDE * CORES), lax.rem(me // CORES, SIDE), lax.rem(me, CORES)
    part = core + CORES * lax.rem(x, 2)

    def at(dz, m):
        away = lax.rem(part + m, PARTS)
        there = ((x // 2) * 2 + away // CORES) * (SIDE * CORES) + y * CORES + lax.rem(away, CORES)
        return (there, lax.rem(z + dz, aux))

    def owner_at(m, k):
        dx, dy, dc = 2 * (k // SIDE) + m // CORES, lax.rem(k, SIDE), m % CORES
        return (
            lax.rem(x + dx, SIDE) * (SIDE * CORES) + lax.rem(y + dy, SIDE) * CORES + lax.rem(core + dc, CORES)
        )

    def load_t2(g):
        return pltpu.make_async_copy(t2_hbm.at[g], t2.at[g], load_sem.at[0, g])

    def load_right(g):
        return pltpu.make_async_copy(right_hbm.at[g], right.at[g], load_sem.at[1, g])

    def load_left(g, k):
        part_of = pl.ds(k * (naux // 4), naux // 4)
        return pltpu.make_async_copy(left_hbm.at[g, part_of], left.at[g, part_of], left_sem.at[g, k])

    def start_loads(g):
        load_t2(g).start()
        for k in range(4):
            load_left(g, k).start()
        load_right(g).start()

    start_loads(0)

    barrier = pltpu.get_barrier_semaphore()
    for dz in (1, 2, 6, 7):
        for m in range(PARTS):
            pl.semaphore_signal(barrier, inc=1, device_id=at(dz, m), device_id_type=MESH)

    def greet(r, carry):
        pl.semaphore_signal(
            barrier, inc=1, device_id=(lax.rem(me + r, owners), z), device_id_type=MESH
        )
        return carry

    lax.fori_loop(1, owners, greet, 0)

    rows_of_info = [
        jnp.full((1, tile), jnp.where(g < count_ref[0], target_ref[g], -1), jnp.int32)
        for g in range(tasks)
    ]
    info[0] = jnp.concatenate(rows_of_info + [jnp.full((8 - tasks, tile), -1, jnp.int32)], axis=0)

    def info_copy(m):
        return pltpu.make_async_remote_copy(
            src_ref=info.at[0], dst_ref=info.at[m], send_sem=info_send.at[m], recv_sem=info_recv.at[m],
            device_id=at(0, m), device_id_type=MESH,
        )

    def relay_copy(p, g):
        dz = (2 + 4 * lax.rem(g, 2), 1, 7)[p]
        return pltpu.make_async_remote_copy(
            src_ref=far_out.at[p, g], dst_ref=relay.at[p, g], send_sem=far_send.at[p, g],
            recv_sem=relay_recv.at[p, g], device_id=at(dz, 0), device_id_type=MESH,
        )

    def near_copy(s, m, g):
        away = lax.rem(part + m, PARTS)
        return pltpu.make_async_remote_copy(
            src_ref=near_out.at[s, g, pl.ds(pl.multiple_of(away * rows, rows), rows)],
            dst_ref=near_in.at[s, m, g], send_sem=near_send.at[s, m, g],
            recv_sem=near_recv.at[s, m, g], device_id=at(NEAR_DZ[s], m), device_id_type=MESH,
        )

    def block_copy(m, k):
        return pltpu.make_async_remote_copy(
            src_ref=blocks_out.at[m, k], dst_ref=blocks_in.at[m, k], send_sem=block_send.at[m, k],
            recv_sem=block_recv.at[m, k], device_id=(owner_at(m, k), z), device_id_type=MESH,
        )

    def amplitudes(u):
        g, stage = lax.rem(u, tasks), u // tasks
        found = []
        for p in range(2):
            a, b, c, d = (pair[p] for pair in OFFSETS)
            low = a + stage * (b - a)
            high = c + (stage - 2) * (d - c)
            offset = low + (stage // 2) * (high - low)
            found.append(t2[g, lax.rem(z + offset, aux)].T)
        return jnp.concatenate(found, axis=0)

    def first(half, u, amps, q):
        g = lax.rem(u, tasks)
        block = lax.dot_general(
            amps, left[g, pl.ds(q, CHUNK)].reshape(CHUNK * tile, tile), (((1,), (1,)), ((), ())),
            preferred_element_type=f32,
        ).astype(bf16)
        for k in range(CHUNK):
            for p in range(2):
                half[(q + k) * tile : (q + k + 1) * tile, p * tile : (p + 1) * tile] = block[
                    p * tile : (p + 1) * tile, k * tile : (k + 1) * tile
                ]

    def second(half, u, q):
        g = lax.rem(u, tasks)
        fit = jnp.concatenate([right[g, q + k] for k in range(CHUNK)], axis=1)
        value = jnp.dot(fit, half[q * tile : (q + CHUNK) * tile, :], preferred_element_type=f32)
        if q == 0:
            term[...] = value
        else:
            term[...] += value

    def wait_first(u):
        @pl.when(u < tasks)
        def _():
            load_t2(u).wait()
            for k in range(4):
                load_left(u, k).wait()

    def wait_second(u):
        @pl.when(u < tasks)
        def _():
            load_right(u).wait()

    def multiply(half_new, half_old, u):
        wait_first(u + 1)

        @pl.when(u < tasks - 2)
        def _():
            start_loads(u + 2)

        wait_second(u)
        amps = amplitudes(u + 1)
        for q in range(0, naux, CHUNK):
            first(half_new, u + 1, amps, q)
            second(half_old, u, q)

    def send_near(s, g, value):
        near_out[s, g] = value.astype(bf16)
        for m in range(PARTS):
            if s < 4 or m:
                near_copy(s, m, g).start()

    def send_relay(p, g, value):
        far_out[p, g] = value.astype(bf16)
        relay_copy(p, g).start()

    def deliver(u):
        g, stage = lax.rem(u, tasks), u // tasks
        lower, upper = slice(0, tile), slice(tile, 2 * tile)

        @pl.when(u == 0)
        def _():
            pl.semaphore_wait(barrier, 4 * PARTS + owners - 1)
            for m in range(1, PARTS):
                info_copy(m).start()

        @pl.when(stage == 0)
        def _():
            send_relay(0, g, term[:, lower])
            send_relay(1, g, term[:, upper])

        @pl.when(stage == 1)
        def _():
            send_relay(2, g, term[:, lower])
            send_near(0, g, term[:, upper])

        @pl.when(stage == 2)
        def _():
            for p in range(3):
                relay_copy(p, g).wait_recv()
            extra = relay[0, g].astype(f32)
            up = (lax.rem(g, 2) == 0).astype(f32)
            send_near(1, g, term[:, lower] + relay[1, g].astype(f32) + extra * up)
            send_near(2, g, term[:, upper] + relay[2, g].astype(f32) + extra * (1.0 - up))

        @pl.when(stage == 3)
        def _():
            send_near(3, g, term[:, lower])
            send_near(4, g, term[:, upper])
            own[g] = term[pl.ds(pl.multiple_of(part * rows, rows), rows), upper]

    def pair_of_units(v, carry):
        multiply(half_odd, half_even, 2 * v)
        deliver(2 * v)
        multiply(half_even, half_odd, 2 * v + 1)
        deliver(2 * v + 1)
        return carry

    load_t2(0).wait()
    amps = amplitudes(0)
    for q in range(0, naux, CHUNK):
        if q % (naux // 4) == 0:
            load_left(0, q // (naux // 4)).wait()
        if q == naux - naux // 4:
            start_loads(1)
        first(half_even, 0, amps, q)
    lax.fori_loop(0, units // 2 - 1, pair_of_units, 0)
    multiply(half_odd, half_even, units - 2)
    deliver(units - 2)
    for q in range(0, naux, CHUNK):
        second(half_odd, units - 1, q)
    deliver(units - 1)

    for m in range(1, PARTS):
        info_copy(m).wait_recv()

    def shares(g):
        found = []
        for m in range(PARTS):
            for s in range(5):
                if s < 4 or m:
                    near_copy(s, m, g).wait_recv()
        for m in range(PARTS):
            value = own[g] if m == 0 else near_in[4, m, g].astype(f32)
            for s in range(4):
                value += near_in[s, m, g].astype(f32)
            found.append(value)
        return found

    def add_shares(g, found, m, k):
        target = owner_at(m, k)
        value = None
        for n in range(PARTS):
            hit = jnp.broadcast_to(info[n, pl.ds(g, 1), :], (rows, tile)) == target
            part_of = jnp.where(hit, found[n], 0.0)
            value = part_of if value is None else value + part_of
        return value

    order = [(m, k) for k in (6, 5, 7, 4, 2, 1, 3, 0) for m in (2, 3, 1, 0)]

    def accumulate(g, carry):
        found = shares(g)
        for m, k in order:
            blocks[m, k] += add_shares(g, found, m, k)
        return carry

    blocks[...] = jnp.zeros_like(blocks)
    lax.fori_loop(0, tasks - 1, accumulate, 0)
    found = shares(tasks - 1)
    for m, k in order:
        value = blocks[m, k] + add_shares(tasks - 1, found, m, k)
        if m or k:
            blocks_out[m, k] = value.astype(bf16)
            block_copy(m, k).start()
        else:
            blocks[0, 0] = value

    for m in range(PARTS):
        for k in range(slots):
            if m or k:
                block_copy(m, k).wait_recv()
        value = None
        for k in range(slots):
            one = blocks[0, 0] if m == 0 and k == 0 else blocks_in[m, k].astype(f32)
            value = one if value is None else value + one
        source = lax.rem(core + m % CORES, CORES) + CORES * lax.rem(x + m // CORES, 2)
        total[pl.ds(pl.multiple_of(source * rows, rows), rows), :] = value
    out_ref[0, 0] = total[...].T.astype(bf16)

    for m in range(1, PARTS):
        info_copy(m).wait_send()

    def finish(g, carry):
        for p in range(3):
            relay_copy(p, g).wait_send()
        for s in range(5):
            for m in range(PARTS):
                if s < 4 or m:
                    near_copy(s, m, g).wait_send()
        return carry

    lax.fori_loop(0, tasks, finish, 0)
    for m in range(PARTS):
        for k in range(slots):
            if m or k:
                block_copy(m, k).wait_send()


def solution(mesh):
    owners, aux = mesh.shape["owner"], mesh.shape["aux"]

    def on_device(fit_left, fit_right, t2_tiles, task_count, task_target):
        tasks, naux, tile, _ = fit_left.shape
        pairs = t2_tiles.shape[1]
        rows = tile // PARTS
        slots = owners // PARTS
        vmem, dma = pltpu.VMEM, pltpu.SemaphoreType.DMA
        return pl.pallas_call(
            functools.partial(kernel, (owners, aux, tasks, naux, tile)),
            out_shape=jax.ShapeDtypeStruct((1, 1, tile, tile), bf16),
            in_specs=[pl.BlockSpec(memory_space=pltpu.SMEM)] * 2 + [pl.BlockSpec(memory_space=pl.ANY)] * 3,
            out_specs=pl.BlockSpec(memory_space=pltpu.VMEM),
            scratch_shapes=[
                vmem((tasks, naux, tile, tile), bf16),
                vmem((tasks, naux, tile, tile), bf16),
                vmem((tasks, pairs, tile, tile), bf16),
                vmem((naux * tile, 2 * tile), bf16),
                vmem((naux * tile, 2 * tile), bf16),
                vmem((tile, 2 * tile), f32),
                vmem((3, tasks, tile, tile), bf16),
                vmem((3, tasks, tile, tile), bf16),
                vmem((5, tasks, tile, tile), bf16),
                vmem((5, PARTS, tasks, rows, tile), bf16),
                vmem((PARTS, 8, tile), jnp.int32),
                vmem((tasks, rows, tile), f32),
                vmem((PARTS, slots, rows, tile), f32),
                vmem((PARTS, slots, rows, tile), bf16),
                vmem((PARTS, slots, rows, tile), bf16),
                vmem((tile, tile), f32),
                dma((2, tasks)),
                dma((tasks, 4)),
                dma((3, tasks)),
                dma((3, tasks)),
                dma((5, PARTS, tasks)),
                dma((5, PARTS, tasks)),
                dma((PARTS,)),
                dma((PARTS,)),
                dma((PARTS, slots)),
                dma((PARTS, slots)),
            ],
            compiler_params=pltpu.CompilerParams(
                collective_id=0, has_side_effects=True, vmem_limit_bytes=62 << 20
            ),
            name="ladder",
        )(task_count, task_target, fit_left, fit_right, t2_tiles)

    placed = (
        P("owner", "aux", None, None),
        P("owner", "aux", None, None),
        P("owner", None, None, None),
        P("owner"),
        P("owner"),
    )
    return jax.shard_map(
        on_device,
        mesh=mesh,
        in_specs=placed,
        out_specs=P("owner", "aux", None, None),
        check_vma=False,
    )
```

```python
import functools

import jax
import jax.numpy as jnp
from jax import lax
from jax.experimental import pallas as pl
from jax.experimental.pallas import tpu as pltpu
from jax.sharding import PartitionSpec as P

MESH = pl.DeviceIdType.MESH
f32, bf16 = jnp.float32, jnp.bfloat16
SIDE, CORES, PARTS, CHUNK = 4, 2, 4, 4
OFFSETS = ((4, 3), (5, 1), (2, 6), (7, 0))
NEAR_DZ = (1, 2, 6, 7, 0)


def kernel(
    sizes, count_ref, target_ref, left_hbm, right_hbm, t2_hbm, out_ref,
    left, right, t2, half_even, half_odd, term, far_out, relay, near_out, near_in, info, own, blocks, blocks_out,
    blocks_in, total,
    load_sem, left_sem, far_send, relay_recv, near_send, near_recv, info_send, info_recv, block_send, block_recv,
):
    owners, aux, tasks, naux, tile = sizes
    rows = tile // PARTS
    units = tasks * len(OFFSETS)
    slots = owners // PARTS
    me = lax.axis_index("owner")
    z = lax.axis_index("aux")
    x, y, core = me // (SIDE * CORES), lax.rem(me // CORES, SIDE), lax.rem(me, CORES)
    part = core + CORES * lax.rem(x, 2)

    def at(dz, m):
        away = lax.rem(part + m, PARTS)
        there = ((x // 2) * 2 + away // CORES) * (SIDE * CORES) + y * CORES + lax.rem(away, CORES)
        return (there, lax.rem(z + dz, aux))

    def owner_at(m, k):
        dx, dy, dc = 2 * (k // SIDE) + m // CORES, lax.rem(k, SIDE), m % CORES
        return (
            lax.rem(x + dx, SIDE) * (SIDE * CORES) + lax.rem(y + dy, SIDE) * CORES + lax.rem(core + dc, CORES)
        )

    def load_t2(g):
        return pltpu.make_async_copy(t2_hbm.at[g], t2.at[g], load_sem.at[0, g])

    def load_right(g):
        return pltpu.make_async_copy(right_hbm.at[g], right.at[g], load_sem.at[1, g])

    def load_left(g, k):
        part_of = pl.ds(k * (naux // 4), naux // 4)
        return pltpu.make_async_copy(left_hbm.at[g, part_of], left.at[g, part_of], left_sem.at[g, k])

    for g in range(tasks):
        load_t2(g).start()
        for k in range(4):
            load_left(g, k).start()
        load_right(g).start()

    barrier = pltpu.get_barrier_semaphore()
    for dz in (1, 2, 6, 7):
        for m in range(PARTS):
            pl.semaphore_signal(barrier, inc=1, device_id=at(dz, m), device_id_type=MESH)

    def greet(r, carry):
        pl.semaphore_signal(
            barrier, inc=1, device_id=(lax.rem(me + r, owners), z), device_id_type=MESH
        )
        return carry

    lax.fori_loop(1, owners, greet, 0)

    rows_of_info = [
        jnp.full((1, tile), jnp.where(g < count_ref[0], target_ref[g], -1), jnp.int32)
        for g in range(tasks)
    ]
    info[0] = jnp.concatenate(rows_of_info + [jnp.full((8 - tasks, tile), -1, jnp.int32)], axis=0)

    def info_copy(m):
        return pltpu.make_async_remote_copy(
            src_ref=info.at[0], dst_ref=info.at[m], send_sem=info_send.at[m], recv_sem=info_recv.at[m],
            device_id=at(0, m), device_id_type=MESH,
        )

    def relay_copy(p, g):
        dz = (2 + 4 * lax.rem(g, 2), 1, 7)[p]
        return pltpu.make_async_remote_copy(
            src_ref=far_out.at[p, g], dst_ref=relay.at[p, g], send_sem=far_send.at[p, g],
            recv_sem=relay_recv.at[p, g], device_id=at(dz, 0), device_id_type=MESH,
        )

    def near_copy(s, m, g):
        away = lax.rem(part + m, PARTS)
        return pltpu.make_async_remote_copy(
            src_ref=near_out.at[s, g, pl.ds(pl.multiple_of(away * rows, rows), rows)],
            dst_ref=near_in.at[s, m, g], send_sem=near_send.at[s, m, g],
            recv_sem=near_recv.at[s, m, g], device_id=at(NEAR_DZ[s], m), device_id_type=MESH,
        )

    def block_copy(m, k):
        return pltpu.make_async_remote_copy(
            src_ref=blocks_out.at[m, k], dst_ref=blocks_in.at[m, k], send_sem=block_send.at[m, k],
            recv_sem=block_recv.at[m, k], device_id=(owner_at(m, k), z), device_id_type=MESH,
        )

    def amplitudes(u):
        g, stage = lax.rem(u, tasks), u // tasks
        found = []
        for p in range(2):
            a, b, c, d = (pair[p] for pair in OFFSETS)
            low = a + stage * (b - a)
            high = c + (stage - 2) * (d - c)
            offset = low + (stage // 2) * (high - low)
            found.append(t2[g, lax.rem(z + offset, aux)].T)
        return jnp.concatenate(found, axis=0)

    def first(half, u, amps, q):
        g = lax.rem(u, tasks)
        block = lax.dot_general(
            amps, left[g, pl.ds(q, CHUNK)].reshape(CHUNK * tile, tile), (((1,), (1,)), ((), ())),
            preferred_element_type=f32,
        ).astype(bf16)
        for k in range(CHUNK):
            for p in range(2):
                half[(q + k) * tile : (q + k + 1) * tile, p * tile : (p + 1) * tile] = block[
                    p * tile : (p + 1) * tile, k * tile : (k + 1) * tile
                ]

    def second(half, u, q):
        g = lax.rem(u, tasks)
        fit = jnp.concatenate([right[g, q + k] for k in range(CHUNK)], axis=1)
        value = jnp.dot(fit, half[q * tile : (q + CHUNK) * tile, :], preferred_element_type=f32)
        if q == 0:
            term[...] = value
        else:
            term[...] += value

    def wait_first(u):
        @pl.when(u < tasks)
        def _():
            load_t2(u).wait()
            for k in range(4):
                load_left(u, k).wait()

    def wait_second(u):
        @pl.when(u < tasks)
        def _():
            load_right(u).wait()

    def multiply(half_new, half_old, u):
        wait_first(u + 1)
        wait_second(u)
        amps = amplitudes(u + 1)
        for q in range(0, naux, CHUNK):
            first(half_new, u + 1, amps, q)
            second(half_old, u, q)

    def send_near(s, g, value):
        near_out[s, g] = value.astype(bf16)
        for m in range(PARTS):
            if s < 4 or m:
                near_copy(s, m, g).start()

    def send_relay(p, g, value):
        far_out[p, g] = value.astype(bf16)
        relay_copy(p, g).start()

    def deliver(u):
        g, stage = lax.rem(u, tasks), u // tasks
        lower, upper = slice(0, tile), slice(tile, 2 * tile)

        @pl.when(u == 0)
        def _():
            pl.semaphore_wait(barrier, 4 * PARTS + owners - 1)
            for m in range(1, PARTS):
                info_copy(m).start()

        @pl.when(stage == 0)
        def _():
            send_relay(0, g, term[:, lower])
            send_relay(1, g, term[:, upper])

        @pl.when(stage == 1)
        def _():
            send_relay(2, g, term[:, lower])
            send_near(0, g, term[:, upper])

        @pl.when(stage == 2)
        def _():
            for p in range(3):
                relay_copy(p, g).wait_recv()
            extra = relay[0, g].astype(f32)
            up = (lax.rem(g, 2) == 0).astype(f32)
            send_near(1, g, term[:, lower] + relay[1, g].astype(f32) + extra * up)
            send_near(2, g, term[:, upper] + relay[2, g].astype(f32) + extra * (1.0 - up))

        @pl.when(stage == 3)
        def _():
            send_near(3, g, term[:, lower])
            send_near(4, g, term[:, upper])
            own[g] = term[pl.ds(pl.multiple_of(part * rows, rows), rows), upper]

    def pair_of_units(v, carry):
        multiply(half_odd, half_even, 2 * v)
        deliver(2 * v)
        multiply(half_even, half_odd, 2 * v + 1)
        deliver(2 * v + 1)
        return carry

    load_t2(0).wait()
    amps = amplitudes(0)
    for q in range(0, naux, CHUNK):
        if q % (naux // 4) == 0:
            load_left(0, q // (naux // 4)).wait()
        first(half_even, 0, amps, q)
    lax.fori_loop(0, units // 2 - 1, pair_of_units, 0)
    multiply(half_odd, half_even, units - 2)
    deliver(units - 2)
    for q in range(0, naux, CHUNK):
        second(half_odd, units - 1, q)
    deliver(units - 1)

    for m in range(1, PARTS):
        info_copy(m).wait_recv()

    def shares(g):
        found = []
        for m in range(PARTS):
            for s in range(5):
                if s < 4 or m:
                    near_copy(s, m, g).wait_recv()
        for m in range(PARTS):
            value = own[g] if m == 0 else near_in[4, m, g].astype(f32)
            for s in range(4):
                value += near_in[s, m, g].astype(f32)
            found.append(value)
        return found

    def add_shares(g, found, m, k):
        target = owner_at(m, k)
        value = None
        for n in range(PARTS):
            hit = jnp.broadcast_to(info[n, pl.ds(g, 1), :], (rows, tile)) == target
            part_of = jnp.where(hit, found[n], 0.0)
            value = part_of if value is None else value + part_of
        return value

    order = [(m, k) for k in (6, 5, 7, 4, 2, 1, 3, 0) for m in (2, 3, 1, 0)]

    def accumulate(g, carry):
        found = shares(g)
        for m, k in order:
            blocks[m, k] += add_shares(g, found, m, k)
        return carry

    blocks[...] = jnp.zeros_like(blocks)
    lax.fori_loop(0, tasks - 1, accumulate, 0)
    found = shares(tasks - 1)
    for m, k in order:
        value = blocks[m, k] + add_shares(tasks - 1, found, m, k)
        if m or k:
            blocks_out[m, k] = value.astype(bf16)
            block_copy(m, k).start()
        else:
            blocks[0, 0] = value

    for m in range(PARTS):
        for k in range(slots):
            if m or k:
                block_copy(m, k).wait_recv()
        value = None
        for k in range(slots):
            one = blocks[0, 0] if m == 0 and k == 0 else blocks_in[m, k].astype(f32)
            value = one if value is None else value + one
        source = lax.rem(core + m % CORES, CORES) + CORES * lax.rem(x + m // CORES, 2)
        total[pl.ds(pl.multiple_of(source * rows, rows), rows), :] = value
    out_ref[0, 0] = total[...].T.astype(bf16)

    for m in range(1, PARTS):
        info_copy(m).wait_send()

    def finish(g, carry):
        for p in range(3):
            relay_copy(p, g).wait_send()
        for s in range(5):
            for m in range(PARTS):
                if s < 4 or m:
                    near_copy(s, m, g).wait_send()
        return carry

    lax.fori_loop(0, tasks, finish, 0)
    for m in range(PARTS):
        for k in range(slots):
            if m or k:
                block_copy(m, k).wait_send()


def solution(mesh):
    owners, aux = mesh.shape["owner"], mesh.shape["aux"]

    def on_device(fit_left, fit_right, t2_tiles, task_count, task_target):
        tasks, naux, tile, _ = fit_left.shape
        pairs = t2_tiles.shape[1]
        rows = tile // PARTS
        slots = owners // PARTS
        vmem, dma = pltpu.VMEM, pltpu.SemaphoreType.DMA
        return pl.pallas_call(
            functools.partial(kernel, (owners, aux, tasks, naux, tile)),
            out_shape=jax.ShapeDtypeStruct((1, 1, tile, tile), bf16),
            in_specs=[pl.BlockSpec(memory_space=pltpu.SMEM)] * 2 + [pl.BlockSpec(memory_space=pl.ANY)] * 3,
            out_specs=pl.BlockSpec(memory_space=pltpu.VMEM),
            scratch_shapes=[
                vmem((tasks, naux, tile, tile), bf16),
                vmem((tasks, naux, tile, tile), bf16),
                vmem((tasks, pairs, tile, tile), bf16),
                vmem((naux * tile, 2 * tile), bf16),
                vmem((naux * tile, 2 * tile), bf16),
                vmem((tile, 2 * tile), f32),
                vmem((3, tasks, tile, tile), bf16),
                vmem((3, tasks, tile, tile), bf16),
                vmem((5, tasks, tile, tile), bf16),
                vmem((5, PARTS, tasks, rows, tile), bf16),
                vmem((PARTS, 8, tile), jnp.int32),
                vmem((tasks, rows, tile), f32),
                vmem((PARTS, slots, rows, tile), f32),
                vmem((PARTS, slots, rows, tile), bf16),
                vmem((PARTS, slots, rows, tile), bf16),
                vmem((tile, tile), f32),
                dma((2, tasks)),
                dma((tasks, 4)),
                dma((3, tasks)),
                dma((3, tasks)),
                dma((5, PARTS, tasks)),
                dma((5, PARTS, tasks)),
                dma((PARTS,)),
                dma((PARTS,)),
                dma((PARTS, slots)),
                dma((PARTS, slots)),
            ],
            compiler_params=pltpu.CompilerParams(
                collective_id=0, has_side_effects=True, vmem_limit_bytes=62 << 20
            ),
            name="ladder",
        )(task_count, task_target, fit_left, fit_right, t2_tiles)

    placed = (
        P("owner", "aux", None, None),
        P("owner", "aux", None, None),
        P("owner", None, None, None),
        P("owner"),
        P("owner"),
    )
    return jax.shard_map(
        on_device,
        mesh=mesh,
        in_specs=placed,
        out_specs=P("owner", "aux", None, None),
        check_vma=False,
    )
```

```python
import functools

import jax
import jax.numpy as jnp
from jax import lax
from jax.experimental import pallas as pl
from jax.experimental.pallas import tpu as pltpu
from jax.sharding import PartitionSpec as P

MESH = pl.DeviceIdType.MESH
f32, bf16 = jnp.float32, jnp.bfloat16
SIDE, CORES, PARTS, CHUNK = 4, 2, 4, 4
OFFSETS = ((4, 3), (5, 1), (2, 6), (7, 0))
NEAR_DZ = (1, 2, 6, 7, 0)
HOLD = 2


def kernel(
    sizes, count_ref, target_ref, left_hbm, right_hbm, t2_hbm, out_ref,
    left, right, t2, half_even, half_odd, term, far_out, relay, near_out, near_in, info, own, blocks, blocks_out,
    blocks_in, total,
    load_sem, left_sem, far_send, relay_recv, near_send, near_recv, info_send, info_recv, block_send, block_recv,
):
    owners, aux, tasks, naux, tile = sizes
    rows = tile // PARTS
    units = tasks * len(OFFSETS)
    slots = owners // PARTS
    me = lax.axis_index("owner")
    z = lax.axis_index("aux")
    x, y, core = me // (SIDE * CORES), lax.rem(me // CORES, SIDE), lax.rem(me, CORES)
    part = core + CORES * lax.rem(x, 2)

    def at(dz, m):
        away = lax.rem(part + m, PARTS)
        there = ((x // 2) * 2 + away // CORES) * (SIDE * CORES) + y * CORES + lax.rem(away, CORES)
        return (there, lax.rem(z + dz, aux))

    def owner_at(m, k):
        dx, dy, dc = 2 * (k // SIDE) + m // CORES, lax.rem(k, SIDE), m % CORES
        return (
            lax.rem(x + dx, SIDE) * (SIDE * CORES) + lax.rem(y + dy, SIDE) * CORES + lax.rem(core + dc, CORES)
        )

    def load_t2(g):
        return pltpu.make_async_copy(t2_hbm.at[g], t2.at[g], load_sem.at[0, g])

    def load_right(g):
        return pltpu.make_async_copy(right_hbm.at[g], right.at[g], load_sem.at[1, g])

    def load_left(g, k):
        part_of = pl.ds(k * (naux // 4), naux // 4)
        return pltpu.make_async_copy(left_hbm.at[g, part_of], left.at[g, part_of], left_sem.at[g, k])

    for g in range(tasks):
        load_t2(g).start()
        for k in range(4):
            load_left(g, k).start()
        load_right(g).start()

    barrier = pltpu.get_barrier_semaphore()
    for dz in (1, 2, 6, 7):
        for m in range(PARTS):
            pl.semaphore_signal(barrier, inc=1, device_id=at(dz, m), device_id_type=MESH)

    def greet(r, carry):
        pl.semaphore_signal(
            barrier, inc=1, device_id=(lax.rem(me + r, owners), z), device_id_type=MESH
        )
        return carry

    lax.fori_loop(1, owners, greet, 0)

    rows_of_info = [
        jnp.full((1, tile), jnp.where(g < count_ref[0], target_ref[g], -1), jnp.int32)
        for g in range(tasks)
    ]
    info[0] = jnp.concatenate(rows_of_info + [jnp.full((8 - tasks, tile), -1, jnp.int32)], axis=0)

    def info_copy(m):
        return pltpu.make_async_remote_copy(
            src_ref=info.at[0], dst_ref=info.at[m], send_sem=info_send.at[m], recv_sem=info_recv.at[m],
            device_id=at(0, m), device_id_type=MESH,
        )

    def relay_copy(p, g):
        dz = (2 + 4 * lax.rem(g, 2), 1, 7)[p]
        return pltpu.make_async_remote_copy(
            src_ref=far_out.at[p, g], dst_ref=relay.at[p, g], send_sem=far_send.at[p, g],
            recv_sem=relay_recv.at[p, g], device_id=at(dz, 0), device_id_type=MESH,
        )

    def near_copy(s, m, g):
        away = lax.rem(part + m, PARTS)
        return pltpu.make_async_remote_copy(
            src_ref=near_out.at[s, g, pl.ds(pl.multiple_of(away * rows, rows), rows)],
            dst_ref=near_in.at[s, m, g], send_sem=near_send.at[s, m, g],
            recv_sem=near_recv.at[s, m, g], device_id=at(NEAR_DZ[s], m), device_id_type=MESH,
        )

    def block_copy(m, k):
        return pltpu.make_async_remote_copy(
            src_ref=blocks_out.at[m, k], dst_ref=blocks_in.at[m, k], send_sem=block_send.at[m, k],
            recv_sem=block_recv.at[m, k], device_id=(owner_at(m, k), z), device_id_type=MESH,
        )

    def amplitudes(u):
        g, stage = lax.rem(u, tasks), u // tasks
        found = []
        for p in range(2):
            a, b, c, d = (pair[p] for pair in OFFSETS)
            low = a + stage * (b - a)
            high = c + (stage - 2) * (d - c)
            offset = low + (stage // 2) * (high - low)
            found.append(t2[g, lax.rem(z + offset, aux)].T)
        return jnp.concatenate(found, axis=0)

    def first(half, u, amps, q):
        g = lax.rem(u, tasks)
        block = lax.dot_general(
            amps, left[g, pl.ds(q, CHUNK)].reshape(CHUNK * tile, tile), (((1,), (1,)), ((), ())),
            preferred_element_type=f32,
        ).astype(bf16)
        for k in range(CHUNK):
            for p in range(2):
                half[(q + k) * tile : (q + k + 1) * tile, p * tile : (p + 1) * tile] = block[
                    p * tile : (p + 1) * tile, k * tile : (k + 1) * tile
                ]

    def second(half, u, q):
        g = lax.rem(u, tasks)
        fit = jnp.concatenate([right[g, q + k] for k in range(CHUNK)], axis=1)
        value = jnp.dot(fit, half[q * tile : (q + CHUNK) * tile, :], preferred_element_type=f32)
        if q == 0:
            term[...] = value
        else:
            term[...] += value

    def wait_first(u):
        @pl.when(u < tasks)
        def _():
            load_t2(u).wait()
            for k in range(4):
                load_left(u, k).wait()

    def wait_second(u):
        @pl.when(u < tasks)
        def _():
            load_right(u).wait()

    def multiply(half_new, half_old, u):
        wait_first(u + 1)
        wait_second(u)
        amps = amplitudes(u + 1)
        for q in range(0, naux, CHUNK):
            first(half_new, u + 1, amps, q)
            second(half_old, u, q)

    def send_near(s, g, value):
        near_out[s, g] = value.astype(bf16)
        for m in range(PARTS):
            if s < 4 or m:
                near_copy(s, m, g).start()

    def send_relay(p, g, value):
        far_out[p, g] = value.astype(bf16)
        relay_copy(p, g).start()

    def deliver(u):
        g, stage = lax.rem(u, tasks), u // tasks
        lower, upper = slice(0, tile), slice(tile, 2 * tile)

        @pl.when(u == HOLD)
        def _():
            pl.semaphore_wait(barrier, 4 * PARTS + owners - 1)
            for m in range(1, PARTS):
                info_copy(m).start()
            for held in range(HOLD):
                relay_copy(0, held).start()
                relay_copy(1, held).start()

        @pl.when(stage == 0)
        def _():
            far_out[0, g] = term[:, lower].astype(bf16)
            far_out[1, g] = term[:, upper].astype(bf16)

            @pl.when(u >= HOLD)
            def _():
                relay_copy(0, g).start()
                relay_copy(1, g).start()

        @pl.when(stage == 1)
        def _():
            send_relay(2, g, term[:, lower])
            send_near(0, g, term[:, upper])

        @pl.when(stage == 2)
        def _():
            for p in range(3):
                relay_copy(p, g).wait_recv()
            extra = relay[0, g].astype(f32)
            up = (lax.rem(g, 2) == 0).astype(f32)
            send_near(1, g, term[:, lower] + relay[1, g].astype(f32) + extra * up)
            send_near(2, g, term[:, upper] + relay[2, g].astype(f32) + extra * (1.0 - up))

        @pl.when(stage == 3)
        def _():
            send_near(3, g, term[:, lower])
            send_near(4, g, term[:, upper])
            own[g] = term[pl.ds(pl.multiple_of(part * rows, rows), rows), upper]

    def pair_of_units(v, carry):
        multiply(half_odd, half_even, 2 * v)
        deliver(2 * v)
        multiply(half_even, half_odd, 2 * v + 1)
        deliver(2 * v + 1)
        return carry

    load_t2(0).wait()
    amps = amplitudes(0)
    for q in range(0, naux, CHUNK):
        if q % (naux // 4) == 0:
            load_left(0, q // (naux // 4)).wait()
        first(half_even, 0, amps, q)
    lax.fori_loop(0, units // 2 - 1, pair_of_units, 0)
    multiply(half_odd, half_even, units - 2)
    deliver(units - 2)
    for q in range(0, naux, CHUNK):
        second(half_odd, units - 1, q)
    deliver(units - 1)

    for m in range(1, PARTS):
        info_copy(m).wait_recv()

    def shares(g):
        found = []
        for m in range(PARTS):
            for s in range(5):
                if s < 4 or m:
                    near_copy(s, m, g).wait_recv()
        for m in range(PARTS):
            value = own[g] if m == 0 else near_in[4, m, g].astype(f32)
            for s in range(4):
                value += near_in[s, m, g].astype(f32)
            found.append(value)
        return found

    def add_shares(g, found, m, k):
        target = owner_at(m, k)
        value = None
        for n in range(PARTS):
            hit = jnp.broadcast_to(info[n, pl.ds(g, 1), :], (rows, tile)) == target
            part_of = jnp.where(hit, found[n], 0.0)
            value = part_of if value is None else value + part_of
        return value

    order = [(m, k) for k in (6, 5, 7, 4, 2, 1, 3, 0) for m in (2, 3, 1, 0)]

    def accumulate(g, carry):
        found = shares(g)
        for m, k in order:
            blocks[m, k] += add_shares(g, found, m, k)
        return carry

    blocks[...] = jnp.zeros_like(blocks)
    lax.fori_loop(0, tasks - 1, accumulate, 0)
    found = shares(tasks - 1)
    for m, k in order:
        value = blocks[m, k] + add_shares(tasks - 1, found, m, k)
        if m or k:
            blocks_out[m, k] = value.astype(bf16)
            block_copy(m, k).start()
        else:
            blocks[0, 0] = value

    for m in range(PARTS):
        for k in range(slots):
            if m or k:
                block_copy(m, k).wait_recv()
        value = None
        for k in range(slots):
            one = blocks[0, 0] if m == 0 and k == 0 else blocks_in[m, k].astype(f32)
            value = one if value is None else value + one
        source = lax.rem(core + m % CORES, CORES) + CORES * lax.rem(x + m // CORES, 2)
        total[pl.ds(pl.multiple_of(source * rows, rows), rows), :] = value
    out_ref[0, 0] = total[...].T.astype(bf16)

    for m in range(1, PARTS):
        info_copy(m).wait_send()

    def finish(g, carry):
        for p in range(3):
            relay_copy(p, g).wait_send()
        for s in range(5):
            for m in range(PARTS):
                if s < 4 or m:
                    near_copy(s, m, g).wait_send()
        return carry

    lax.fori_loop(0, tasks, finish, 0)
    for m in range(PARTS):
        for k in range(slots):
            if m or k:
                block_copy(m, k).wait_send()


def solution(mesh):
    owners, aux = mesh.shape["owner"], mesh.shape["aux"]

    def on_device(fit_left, fit_right, t2_tiles, task_count, task_target):
        tasks, naux, tile, _ = fit_left.shape
        pairs = t2_tiles.shape[1]
        rows = tile // PARTS
        slots = owners // PARTS
        vmem, dma = pltpu.VMEM, pltpu.SemaphoreType.DMA
        return pl.pallas_call(
            functools.partial(kernel, (owners, aux, tasks, naux, tile)),
            out_shape=jax.ShapeDtypeStruct((1, 1, tile, tile), bf16),
            in_specs=[pl.BlockSpec(memory_space=pltpu.SMEM)] * 2 + [pl.BlockSpec(memory_space=pl.ANY)] * 3,
            out_specs=pl.BlockSpec(memory_space=pltpu.VMEM),
            scratch_shapes=[
                vmem((tasks, naux, tile, tile), bf16),
                vmem((tasks, naux, tile, tile), bf16),
                vmem((tasks, pairs, tile, tile), bf16),
                vmem((naux * tile, 2 * tile), bf16),
                vmem((naux * tile, 2 * tile), bf16),
                vmem((tile, 2 * tile), f32),
                vmem((3, tasks, tile, tile), bf16),
                vmem((3, tasks, tile, tile), bf16),
                vmem((5, tasks, tile, tile), bf16),
                vmem((5, PARTS, tasks, rows, tile), bf16),
                vmem((PARTS, 8, tile), jnp.int32),
                vmem((tasks, rows, tile), f32),
                vmem((PARTS, slots, rows, tile), f32),
                vmem((PARTS, slots, rows, tile), bf16),
                vmem((PARTS, slots, rows, tile), bf16),
                vmem((tile, tile), f32),
                dma((2, tasks)),
                dma((tasks, 4)),
                dma((3, tasks)),
                dma((3, tasks)),
                dma((5, PARTS, tasks)),
                dma((5, PARTS, tasks)),
                dma((PARTS,)),
                dma((PARTS,)),
                dma((PARTS, slots)),
                dma((PARTS, slots)),
            ],
            compiler_params=pltpu.CompilerParams(
                collective_id=0, has_side_effects=True, vmem_limit_bytes=62 << 20
            ),
            name="ladder",
        )(task_count, task_target, fit_left, fit_right, t2_tiles)

    placed = (
        P("owner", "aux", None, None),
        P("owner", "aux", None, None),
        P("owner", None, None, None),
        P("owner"),
        P("owner"),
    )
    return jax.shard_map(
        on_device,
        mesh=mesh,
        in_specs=placed,
        out_specs=P("owner", "aux", None, None),
        check_vma=False,
    )
```
